32 devices in a mesh: group: 2 (over y), patch: 4 (over z), head: 2 (over x), sub: 2 (over core).
Axes of the slice: x: 2, y: 2, z: 4, core: 2. Of those that a mesh axis runs over, the one named last changes fastest.
Arguments:
- qkv: bfloat16 [3, 16, 128, 3072], P(None, ('group', 'patch', 'sub'), 'head'), parts along dimension 1, may hold values from -64 to 64
- stale_kv: bfloat16 [2, 16, 128, 3072], P(None, ('group', 'patch', 'sub'), None, 'head'), parts along dimension 1, may hold values from -6 to 6
- w_out: bfloat16 [3072, 3072], P('head'), may hold values from -0.109375 to 0.109375
- neighbors: int32 [32, 6], P(('group', 'patch', 'sub')), parts along dimension 0, may hold values from 0 to 15, as said below
Outputs:
- block_output: bfloat16 [16, 128, 3072], P(('group', 'patch', 'sub'), 'head'), parts along dimension 0
The draws below stay inside these ranges and needn't reach their ends.
There are 2 independent parts, one for each index of `group`. The reference program is written for one: setup_inputs(seed, part) draws one part's arguments, and reference() takes and returns one part's arrays. A program takes and returns all parts, laid end to end along the dimension named above; an argument that names none is the same for every part. Nothing has to cross between parts.
Inputs may be any that keep to these rules, and one draw needn't show every extreme that they name: `neighbors`: row g lists 6 distinct blocks; the first is g itself, the others lie within 3 block rows and one block column of g, where block g has block row g // 2 and block column g % 2.
All inputs are finite; a program needn't handle non-finite values.
Results may differ from the reference program's by a relative error of at most 0.0066.
Values may be sent and summed in bfloat16 or wider, within the bound.
A program may use at most 64 MiB of HBM per device.

```python
import math
import jax
import jax.numpy as jnp
from jax import lax

D = 3072
H = 24
HD = 128
BLOCK = 64
NB = 6
REACH = 3
TOK_SHARD = 128
SHARDS = 8
BPS = 2
NBLK = 16
N_HEAD = 2


def draw_qkv(key, part):
    key = jax.random.fold_in(key, 11)
    shape = (3, SHARDS, TOK_SHARD, D)
    full = jnp.clip(jax.random.normal(jax.random.fold_in(key, 1), shape, jnp.float32), -6.0, 6.0)
    return full.astype(jnp.bfloat16)


def draw_neighbors(key, part):
    key = jax.random.fold_in(key, 7)
    blocks = jnp.arange(NBLK, dtype=jnp.int32)
    row = blocks // BPS
    column = blocks % BPS
    row_steps = jnp.repeat(jnp.arange(-REACH, REACH + 1, dtype=jnp.int32), 3)
    col_steps = jnp.tile(jnp.arange(-1, 2, dtype=jnp.int32), 2 * REACH + 1)
    count = (2 * REACH + 1) * 3
    rows = row[:, None] + row_steps[None, :]
    cols = column[:, None] + col_steps[None, :]
    valid = (rows >= 0) & (rows < SHARDS) & (cols >= 0) & (cols < BPS)
    valid = valid & ~((row_steps == 0) & (col_steps == 0))[None, :]
    scores = jax.random.randint(key, (NBLK, count), 0, 2 ** 20) * 32 + jnp.arange(count, dtype=jnp.int32)[None, :]
    scores = jnp.where(valid, scores, 2 ** 30)
    order = jnp.argsort(scores, axis=1, stable=True)[:, :NB - 1]
    ids = rows * BPS + cols
    picked = jnp.take_along_axis(ids, order, axis=1)
    return jnp.concatenate([blocks[:, None], picked], axis=1).astype(jnp.int32)


def steps_of(stream_key, shape, cuts, smallest, high):
    factor_of = 1.0
    for dim, parts in cuts:
        draws = jax.random.uniform(jax.random.fold_in(jax.random.fold_in(stream_key, 6), dim), (parts,), jnp.float32, smallest / len(cuts), high / len(cuts))
        factor_of = factor_of * jnp.repeat(jnp.exp(draws), shape[dim] // parts).reshape((-1,) + (1,) * (len(shape) - 1 - dim))
    return factor_of


def centred(rng, extent, deviation, limit, pieces=(), held_as=jnp.bfloat16):
    result = deviation * jax.random.normal(rng, extent, jnp.float32)
    if pieces:
        result = result * steps_of(rng, extent, pieces, -0.22, 0.18)
    return jnp.clip(result, -limit, limit).astype(held_as)


def setup_inputs(seed: int = 0, part: int = 0) -> dict:
    streams_of = jax.random.split(jax.random.key(seed), 5)
    part_splits = jax.random.split(jax.random.fold_in(streams_of[4], part), 5)
    qkv = draw_qkv(jax.random.fold_in(jax.random.fold_in(streams_of[4], part), 71), part)
    stale_kv = centred(part_splits[1], (2, SHARDS, TOK_SHARD, D), 1.0, 6.0, ((1, 8), (3, 2)))
    w_out = centred(streams_of[2], (D, D), D ** -0.5, 0.109375, ((0, 2),))
    neighbors = draw_neighbors(jax.random.fold_in(jax.random.fold_in(streams_of[4], part), 71), part)
    return {"qkv": qkv, "stale_kv": stale_kv, "w_out": w_out, "neighbors": neighbors}


def reference(qkv, stale_kv, w_out, neighbors):
    local_heads = H // N_HEAD
    width = local_heads * HD
    fresh = qkv[1:3].reshape(2, NBLK, BLOCK, D)
    stale = stale_kv.reshape(2, NBLK, BLOCK, D)
    queries = qkv[0].reshape(SHARDS, BPS, BLOCK, H, HD)
    w_groups = w_out.reshape(N_HEAD, width, D).astype(jnp.float32)

    def one_shard(shard):
        listed = lax.dynamic_slice_in_dim(neighbors, (shard * BPS).astype(jnp.int32), BPS, 0)
        same_row = listed // BPS == shard
        picked = jnp.where(same_row[None, :, :, None, None], fresh[:, listed], stale[:, listed])
        picked = picked.reshape(2, BPS, NB * BLOCK, H, HD)
        query = queries[shard].astype(jnp.float32)
        scores = jnp.einsum('bqhd,bkhd->bhqk', query, picked[0].astype(jnp.float32)) / math.sqrt(HD)
        top = lax.optimization_barrier(jnp.max(scores, axis=-1, keepdims=True))
        expo = jnp.exp(scores - top)
        weights = (expo / lax.optimization_barrier(jnp.sum(expo, axis=-1, keepdims=True))).astype(jnp.bfloat16)
        attended = jnp.einsum('bhqk,bkhd->bqhd', weights.astype(jnp.float32), picked[1].astype(jnp.float32))
        attended = attended.astype(jnp.bfloat16).reshape(TOK_SHARD, N_HEAD, width)
        partials = jnp.einsum('tgc,gce->gte', attended.astype(jnp.float32), w_groups).astype(jnp.bfloat16)
        partials = lax.optimization_barrier(partials)
        return lax.optimization_barrier(jnp.sum(partials.astype(jnp.float32), axis=0)).astype(jnp.bfloat16)
    return lax.map(one_shard, jnp.arange(SHARDS, dtype=jnp.int32))
```

```python
import functools
import math

import jax
import jax.numpy as jnp
from jax import lax
from jax.experimental import pallas as pl
from jax.experimental.pallas import tpu as pltpu
from jax.sharding import PartitionSpec as P

HD = 128
BLOCK = 64
NB = 6
REACH = 3
MESH = pl.DeviceIdType.MESH


def head_cuts(local_heads):
    if local_heads % 4 == 0:
        return [4] * (local_heads // 4)
    return [1] * local_heads


def column_piece(total):
    for size in (768, 512, 256, 128):
        if total % size == 0:
            return size
    return total


def kernel(
    heads, chips, cuts, piece,
    near_ref, qkv_ref, stale_ref, w_ref, out_ref,
    w_buf, acc, att, sent, landed, banks, asked,
    w_sem, fill_send, fill_recv, own_send, bank_recv, bank_send, part_send, part_recv,
):
    z = lax.axis_index("patch")
    h = lax.axis_index("head")
    s = lax.axis_index("sub")
    row = 2 * z + s
    blocks = stale_ref.shape[1]
    rows = qkv_ref.shape[2]
    width = stale_ref.shape[3]
    depth = out_ref.shape[2]
    has_left = z > 0
    has_right = z < chips - 1
    core0 = s == 0
    has_diag = jnp.logical_or(jnp.logical_and(core0, has_left), jnp.logical_and(s == 1, has_right))
    diag_z = jnp.where(core0, jnp.maximum(z - 1, 0), jnp.minimum(z + 1, chips - 1))
    left = {"patch": jnp.maximum(z - 1, 0)}
    right = {"patch": jnp.minimum(z + 1, chips - 1)}
    sibling = {"sub": 1 - s}
    diag = {"patch": diag_z, "sub": 1 - s}
    peers = [lax.rem(h + k, heads) for k in range(1, heads)]
    sources = [lax.rem(h - k + heads, heads) for k in range(1, heads)]

    barrier = pltpu.get_barrier_semaphore()

    @pl.when(has_left)
    def _():
        pl.semaphore_signal(barrier, inc=1, device_id=left, device_id_type=MESH)

    @pl.when(has_right)
    def _():
        pl.semaphore_signal(barrier, inc=1, device_id=right, device_id_type=MESH)

    @pl.when(has_diag)
    def _():
        pl.semaphore_signal(barrier, inc=1, device_id=diag, device_id_type=MESH)

    pl.semaphore_signal(barrier, inc=1, device_id=sibling, device_id_type=MESH)
    for peer in peers:
        pl.semaphore_signal(barrier, inc=1, device_id={"head": peer}, device_id_type=MESH)

    starts = [sum(cuts[:c]) * HD for c in range(len(cuts))]

    def row_at(c, slot):
        return banks[c].at[:, pl.ds(slot * blocks, blocks)]

    def remote(src, dst, send, recv, device):
        return pltpu.make_async_remote_copy(
            src_ref=src, dst_ref=dst, send_sem=send, recv_sem=recv,
            device_id=device, device_id_type=MESH,
        )

    def fresh_dst(c, owner):
        first = owner * rows
        block = REACH * blocks + first // BLOCK
        inside = pl.multiple_of(first % BLOCK, rows)
        return (
            asked[c].at[pl.ds(pl.multiple_of(first, rows), rows)],
            banks[c].at[:, block, pl.ds(inside, rows)],
        )

    def fresh_src(c, owner):
        cols = pl.ds(pl.multiple_of(owner * width + starts[c], HD), cuts[c] * HD)
        return qkv_ref.at[0, 0, :, cols], qkv_ref.at[1:3, 0, :, cols]

    def local_fill(c):
        src, dst = fresh_src(c, h), fresh_dst(c, h)
        return [pltpu.make_async_copy(src[i], dst[i], w_sem.at[1 + i, c]) for i in range(2)]

    def w_fill(c):
        part = pl.ds(starts[c], cuts[c] * HD)
        return pltpu.make_async_copy(w_ref.at[part], w_buf.at[part], w_sem.at[0, c])

    def fresh_to(c, k):
        src, dst = fresh_src(c, peers[k]), fresh_dst(c, h)
        return [
            remote(src[i], dst[i], fill_send.at[c, k, i], fill_recv.at[c, k, i], {"head": peers[k]})
            for i in range(2)
        ]

    def fresh_from(c, k):
        src, dst = fresh_src(c, h), fresh_dst(c, sources[k])
        return [
            remote(src[i], dst[i], fill_send.at[c, k, i], fill_recv.at[c, k, i], {"head": peers[k]})
            for i in range(2)
        ]

    def own(c):
        return stale_ref.at[:, :, :, starts[c]:starts[c] + cuts[c] * HD]

    def to_right(c):
        return remote(own(c), row_at(c, 1), own_send.at[c, 0], bank_recv.at[c, 0], right)

    def to_left(c):
        return remote(own(c), row_at(c, 5), own_send.at[c, 1], bank_recv.at[c, 1], left)

    sib_own = jnp.where(core0, 2, 4)
    sib_left = jnp.where(core0, 0, 2)
    sib_right = jnp.where(core0, 4, 6)
    my_own = jnp.where(core0, 4, 2)
    my_left = jnp.where(core0, 2, 0)
    my_right = jnp.where(core0, 6, 4)

    def own_sib(c, slot):
        return remote(own(c), row_at(c, slot), own_send.at[c, 2], bank_recv.at[c, 2], sibling)

    def left_sib(c, slot):
        return remote(row_at(c, 1), row_at(c, slot), bank_send.at[c, 0], bank_recv.at[c, 3], sibling)

    def right_sib(c, slot):
        return remote(row_at(c, 5), row_at(c, slot), bank_send.at[c, 1], bank_recv.at[c, 4], sibling)

    def far(c, src, dst):
        return remote(row_at(c, src), row_at(c, dst), bank_send.at[c, 2], bank_recv.at[c, 5], diag)

    inner = jnp.logical_and(has_left, has_right)
    far_src = jnp.where(core0, 5, 1)
    far_dst = jnp.where(core0, 6, 0)
    far_mine = jnp.where(core0, 0, 6)
    has_far = jnp.logical_or(jnp.logical_and(core0, z >= 2), jnp.logical_and(s == 1, z <= chips - 3))

    for c in range(len(cuts)):
        for copy in local_fill(c):
            copy.start()
        w_fill(c).start()

    count = (
        heads + has_left.astype(jnp.int32) + has_right.astype(jnp.int32) + has_diag.astype(jnp.int32)
    )
    pl.semaphore_wait(barrier, count)

    for c in range(len(cuts)):
        @pl.when(has_right)
        def _():
            to_right(c).start()

        @pl.when(has_left)
        def _():
            to_left(c).start()

        for k in range(heads - 1):
            for copy in fresh_to(c, k):
                copy.start()
        own_sib(c, sib_own).start()

    def pass_on(c):
        @pl.when(has_left)
        def _():
            to_left_arrived = remote(own(c), row_at(c, 1), own_send.at[c, 0], bank_recv.at[c, 0], right)
            to_left_arrived.wait_recv()

        @pl.when(has_right)
        def _():
            remote(own(c), row_at(c, 5), own_send.at[c, 1], bank_recv.at[c, 1], left).wait_recv()

        @pl.when(inner)
        def _():
            far(c, far_src, far_dst).start()

        @pl.when(has_left)
        def _():
            left_sib(c, sib_left).start()

        @pl.when(has_right)
        def _():
            right_sib(c, sib_right).start()

    def arrived(c):
        for copy in local_fill(c):
            copy.wait()
        for k in range(heads - 1):
            for copy in fresh_from(c, k):
                copy.wait_recv()
        own_sib(c, my_own).wait_recv()

        @pl.when(has_left)
        def _():
            left_sib(c, my_left).wait_recv()

        @pl.when(has_right)
        def _():
            right_sib(c, my_right).wait_recv()

        @pl.when(has_far)
        def _():
            far(c, far_src, far_mine).wait_recv()

    first_block = (row - REACH) * blocks
    scale = 1.0 / math.sqrt(HD)

    def attend(c):
        for b in range(blocks):
            listed = [
                jnp.clip(near_ref[b, n] - first_block, 0, banks[c].shape[1] - 1) for n in range(NB)
            ]
            for head in range(cuts[c]):
                cols = slice(head * HD, (head + 1) * HD)
                query = asked[c][b * BLOCK:(b + 1) * BLOCK, cols]
                keys = jnp.concatenate([banks[c][0, n, :, cols] for n in listed], axis=0)
                values = jnp.concatenate([banks[c][1, n, :, cols] for n in listed], axis=0)
                scores = lax.dot_general(
                    query, keys, (((1,), (1,)), ((), ())), preferred_element_type=jnp.float32
                ) * scale
                top = jnp.max(scores, axis=-1, keepdims=True)
                expo = jnp.exp(scores - top)
                weights = (expo * (1.0 / jnp.sum(expo, axis=-1, keepdims=True))).astype(jnp.bfloat16)
                got = jnp.dot(weights, values, preferred_element_type=jnp.float32)
                att[b * BLOCK:(b + 1) * BLOCK, starts[c] + head * HD:starts[c] + (head + 1) * HD] = (
                    got.astype(jnp.bfloat16)
                )

    def product(c, columns):
        part = slice(starts[c], starts[c] + cuts[c] * HD)
        return jnp.dot(att[:, part], w_buf[part, columns], preferred_element_type=jnp.float32)

    def project(c):
        w_fill(c).wait()

        @pl.loop(0, depth // piece)
        def _(j):
            columns = pl.ds(pl.multiple_of(j * piece, piece), piece)
            if c == 0:
                acc[:, columns] = product(c, columns)
            else:
                acc[:, columns] += product(c, columns)

    last = len(cuts) - 1
    pass_on(0)
    for c in range(last):
        pass_on(c + 1)
        arrived(c)
        attend(c)
        project(c)
    arrived(last)
    attend(last)
    w_fill(last).wait()

    def part_to(j, k):
        columns = slice(j * piece, (j + 1) * piece)
        mine = pl.ds(pl.multiple_of(peers[k] * rows, rows), rows)
        return remote(
            sent.at[mine, columns], landed.at[k, :, columns],
            part_send.at[k, j], part_recv.at[k, j], {"head": peers[k]},
        )

    for j in range(depth // piece):
        columns = slice(j * piece, (j + 1) * piece)
        total = product(last, columns)
        if last > 0:
            total = total + acc[:, columns]
        sent[:, columns] = total.astype(jnp.bfloat16)
        for k in range(heads - 1):
            part_to(j, k).start()

    own_rows = pl.ds(pl.multiple_of(h * rows, rows), rows)
    for j in range(depth // piece):
        columns = slice(j * piece, (j + 1) * piece)
        total = sent[own_rows, columns].astype(jnp.float32)
        for k in range(heads - 1):
            part_to(j, k).wait_recv()
            total = total + landed[k, :, columns].astype(jnp.float32)
        out_ref[0, :, columns] = total.astype(jnp.bfloat16)

    for c in range(len(cuts)):
        @pl.when(has_right)
        def _():
            to_right(c).wait_send()
            right_sib(c, sib_right).wait_send()

        @pl.when(has_left)
        def _():
            to_left(c).wait_send()
            left_sib(c, sib_left).wait_send()

        @pl.when(inner)
        def _():
            far(c, far_src, far_dst).wait_send()

        own_sib(c, sib_own).wait_send()
        for k in range(heads - 1):
            for copy in fresh_to(c, k):
                copy.wait_send()
    for j in range(depth // piece):
        for k in range(heads - 1):
            part_to(j, k).wait_send()


def per_device(heads, chips, qkv, stale_kv, w_out, neighbors):
    rows = qkv.shape[2]
    tokens = stale_kv.shape[2]
    width, depth = w_out.shape
    blocks = tokens // BLOCK
    cuts = head_cuts(width // HD)
    piece = column_piece(depth)
    pieces = depth // piece
    others = heads - 1
    count = len(cuts)
    bf16 = jnp.bfloat16
    stale = stale_kv.reshape(2, blocks, BLOCK, width)
    slots = (2 * REACH + 1) * blocks
    dma = pltpu.SemaphoreType.DMA
    return pl.pallas_call(
        functools.partial(kernel, heads, chips, cuts, piece),
        out_shape=jax.ShapeDtypeStruct((1, rows, depth), bf16),
        in_specs=[
            pl.BlockSpec(memory_space=pltpu.SMEM),
            pl.BlockSpec(memory_space=pl.ANY),
            pl.BlockSpec(memory_space=pl.ANY),
            pl.BlockSpec(memory_space=pl.ANY),
        ],
        out_specs=pl.BlockSpec(memory_space=pltpu.VMEM),
        scratch_shapes=[
            pltpu.VMEM((width, depth), bf16),
            pltpu.VMEM((tokens, depth), jnp.float32),
            pltpu.VMEM((tokens, width), bf16),
            pltpu.VMEM((tokens, depth), bf16),
            pltpu.VMEM((others, rows, depth), bf16),
            [pltpu.VMEM((2, slots, BLOCK, cut * HD), bf16) for cut in cuts],
            [pltpu.VMEM((tokens, cut * HD), bf16) for cut in cuts],
            dma((3, count)),
            dma((count, others, 2)),
            dma((count, others, 2)),
            dma((count, 3)),
            dma((count, 6)),
            dma((count, 3)),
            dma((others, pieces)),
            dma((others, pieces)),
        ],
        compiler_params=pltpu.CompilerParams(
            collective_id=0, has_side_effects=True, vmem_limit_bytes=48 * 2 ** 20
        ),
        name="windowed",
    )(neighbors, qkv, stale, w_out)


def solution(mesh):
    placed = (
        P(None, ("group", "patch", "sub"), "head", None),
        P(None, ("group", "patch", "sub"), None, "head"),
        P("head", None),
        P(("group", "patch", "sub"), None),
    )
    sizes = dict(mesh.shape)
    return jax.shard_map(
        functools.partial(per_device, sizes["head"], sizes["patch"]),
        mesh=mesh,
        in_specs=placed,
        out_specs=P(("group", "patch", "sub"), "head", None),
        check_vma=False,
    )
```

```python
import functools
import math

import jax
import jax.numpy as jnp
from jax import lax
from jax.experimental import pallas as pl
from jax.experimental.pallas import tpu as pltpu
from jax.sharding import PartitionSpec as P

HD = 128
BLOCK = 64
NB = 6
REACH = 3
MESH = pl.DeviceIdType.MESH


def head_cuts(local_heads):
    if local_heads % 6 == 0:
        return [6] * (local_heads // 6)
    return [1] * local_heads


def column_piece(total):
    for size in (768, 512, 256, 128):
        if total % size == 0:
            return size
    return total


def kernel(
    heads, chips, cuts, piece,
    near_ref, qkv_ref, stale_ref, w_ref, out_ref,
    w_buf, acc, att, sent, landed, banks, asked,
    w_sem, fill_send, fill_recv, own_send, bank_recv, bank_send, part_send, part_recv,
):
    z = lax.axis_index("patch")
    h = lax.axis_index("head")
    s = lax.axis_index("sub")
    row = 2 * z + s
    blocks = stale_ref.shape[1]
    rows = qkv_ref.shape[2]
    width = stale_ref.shape[3]
    depth = out_ref.shape[2]
    has_left = z > 0
    has_right = z < chips - 1
    core0 = s == 0
    has_diag = jnp.logical_or(jnp.logical_and(core0, has_left), jnp.logical_and(s == 1, has_right))
    diag_z = jnp.where(core0, jnp.maximum(z - 1, 0), jnp.minimum(z + 1, chips - 1))
    left = {"patch": jnp.maximum(z - 1, 0)}
    right = {"patch": jnp.minimum(z + 1, chips - 1)}
    sibling = {"sub": 1 - s}
    diag = {"patch": diag_z, "sub": 1 - s}
    peers = [lax.rem(h + k, heads) for k in range(1, heads)]
    sources = [lax.rem(h - k + heads, heads) for k in range(1, heads)]

    barrier = pltpu.get_barrier_semaphore()

    @pl.when(has_left)
    def _():
        pl.semaphore_signal(barrier, inc=1, device_id=left, device_id_type=MESH)

    @pl.when(has_right)
    def _():
        pl.semaphore_signal(barrier, inc=1, device_id=right, device_id_type=MESH)

    @pl.when(has_diag)
    def _():
        pl.semaphore_signal(barrier, inc=1, device_id=diag, device_id_type=MESH)

    pl.semaphore_signal(barrier, inc=1, device_id=sibling, device_id_type=MESH)
    for peer in peers:
        pl.semaphore_signal(barrier, inc=1, device_id={"head": peer}, device_id_type=MESH)

    starts = [sum(cuts[:c]) * HD for c in range(len(cuts))]

    def row_at(c, slot):
        return banks[c].at[:, pl.ds(slot * blocks, blocks)]

    def remote(src, dst, send, recv, device):
        return pltpu.make_async_remote_copy(
            src_ref=src, dst_ref=dst, send_sem=send, recv_sem=recv,
            device_id=device, device_id_type=MESH,
        )

    def fresh_dst(c, owner):
        first = owner * rows
        block = REACH * blocks + first // BLOCK
        inside = pl.multiple_of(first % BLOCK, rows)
        return (
            asked[c].at[pl.ds(pl.multiple_of(first, rows), rows)],
            banks[c].at[:, block, pl.ds(inside, rows)],
        )

    def fresh_src(c, owner):
        cols = pl.ds(pl.multiple_of(owner * width + starts[c], HD), cuts[c] * HD)
        return qkv_ref.at[0, 0, :, cols], qkv_ref.at[1:3, 0, :, cols]

    def local_fill(c):
        src, dst = fresh_src(c, h), fresh_dst(c, h)
        return [pltpu.make_async_copy(src[i], dst[i], w_sem.at[1 + i, c]) for i in range(2)]

    def w_fill(c):
        part = pl.ds(starts[c], cuts[c] * HD)
        return pltpu.make_async_copy(w_ref.at[part], w_buf.at[part], w_sem.at[0, c])

    def fresh_to(c, k):
        src, dst = fresh_src(c, peers[k]), fresh_dst(c, h)
        return [
            remote(src[i], dst[i], fill_send.at[c, k, i], fill_recv.at[c, k, i], {"head": peers[k]})
            for i in range(2)
        ]

    def fresh_from(c, k):
        src, dst = fresh_src(c, h), fresh_dst(c, sources[k])
        return [
            remote(src[i], dst[i], fill_send.at[c, k, i], fill_recv.at[c, k, i], {"head": peers[k]})
            for i in range(2)
        ]

    def own(c):
        return stale_ref.at[:, :, :, starts[c]:starts[c] + cuts[c] * HD]

    def to_right(c):
        return remote(own(c), row_at(c, 1), own_send.at[c, 0], bank_recv.at[c, 0], right)

    def to_left(c):
        return remote(own(c), row_at(c, 5), own_send.at[c, 1], bank_recv.at[c, 1], left)

    sib_own = jnp.where(core0, 2, 4)
    sib_left = jnp.where(core0, 0, 2)
    sib_right = jnp.where(core0, 4, 6)
    my_own = jnp.where(core0, 4, 2)
    my_left = jnp.where(core0, 2, 0)
    my_right = jnp.where(core0, 6, 4)

    def own_sib(c, slot):
        return remote(own(c), row_at(c, slot), own_send.at[c, 2], bank_recv.at[c, 2], sibling)

    def left_sib(c, slot):
        return remote(row_at(c, 1), row_at(c, slot), bank_send.at[c, 0], bank_recv.at[c, 3], sibling)

    def right_sib(c, slot):
        return remote(row_at(c, 5), row_at(c, slot), bank_send.at[c, 1], bank_recv.at[c, 4], sibling)

    def far(c, src, dst):
        return remote(row_at(c, src), row_at(c, dst), bank_send.at[c, 2], bank_recv.at[c, 5], diag)

    inner = jnp.logical_and(has_left, has_right)
    far_src = jnp.where(core0, 5, 1)
    far_dst = jnp.where(core0, 6, 0)
    far_mine = jnp.where(core0, 0, 6)
    has_far = jnp.logical_or(jnp.logical_and(core0, z >= 2), jnp.logical_and(s == 1, z <= chips - 3))

    for c in range(len(cuts)):
        for copy in local_fill(c):
            copy.start()
        w_fill(c).start()

    count = (
        heads + has_left.astype(jnp.int32) + has_right.astype(jnp.int32) + has_diag.astype(jnp.int32)
    )
    pl.semaphore_wait(barrier, count)

    for c in range(len(cuts)):
        @pl.when(has_right)
        def _():
            to_right(c).start()

        @pl.when(has_left)
        def _():
            to_left(c).start()

        for k in range(heads - 1):
            for copy in fresh_to(c, k):
                copy.start()
        own_sib(c, sib_own).start()

    def pass_on(c):
        @pl.when(has_left)
        def _():
            to_left_arrived = remote(own(c), row_at(c, 1), own_send.at[c, 0], bank_recv.at[c, 0], right)
            to_left_arrived.wait_recv()

        @pl.when(has_right)
        def _():
            remote(own(c), row_at(c, 5), own_send.at[c, 1], bank_recv.at[c, 1], left).wait_recv()

        @pl.when(inner)
        def _():
            far(c, far_src, far_dst).start()

        @pl.when(has_left)
        def _():
            left_sib(c, sib_left).start()

        @pl.when(has_right)
        def _():
            right_sib(c, sib_right).start()

    def arrived(c):
        for copy in local_fill(c):
            copy.wait()
        for k in range(heads - 1):
            for copy in fresh_from(c, k):
                copy.wait_recv()
        own_sib(c, my_own).wait_recv()

        @pl.when(has_left)
        def _():
            left_sib(c, my_left).wait_recv()

        @pl.when(has_right)
        def _():
            right_sib(c, my_right).wait_recv()

        @pl.when(has_far)
        def _():
            far(c, far_src, far_mine).wait_recv()

    first_block = (row - REACH) * blocks
    scale = math.log2(math.e) / math.sqrt(HD)

    def attend(c, b):
        tokens = pl.ds(pl.multiple_of(b * BLOCK, BLOCK), BLOCK)
        most = banks[c].shape[1] - 1
        listed = [jnp.clip(near_ref[b, n] - first_block, 0, most) for n in range(NB)]
        spans = [slice(head * HD, (head + 1) * HD) for head in range(cuts[c])]
        scores = [
            lax.dot_general(
                asked[c][tokens, cols],
                jnp.concatenate([banks[c][0, n, :, cols] for n in listed], axis=0),
                (((1,), (1,)), ((), ())),
                preferred_element_type=jnp.float32,
            )
            for cols in spans
        ]
        tops = [jnp.max(score, axis=-1, keepdims=True) for score in scores]
        expos = [jnp.exp2((score - top) * scale) for score, top in zip(scores, tops)]
        got = [
            jnp.dot(
                expo.astype(jnp.bfloat16),
                jnp.concatenate([banks[c][1, n, :, cols] for n in listed], axis=0),
                preferred_element_type=jnp.float32,
            )
            for expo, cols in zip(expos, spans)
        ]
        sums = [jnp.sum(expo, axis=-1, keepdims=True) for expo in expos]
        for head in range(cuts[c]):
            first = starts[c] + head * HD
            att[tokens, first:first + HD] = (got[head] * (1.0 / sums[head])).astype(jnp.bfloat16)

    def product(c, tokens, columns):
        part = slice(starts[c], starts[c] + cuts[c] * HD)
        return jnp.dot(att[tokens, part], w_buf[part, columns], preferred_element_type=jnp.float32)

    def project(c):
        w_fill(c).wait()

        @pl.loop(0, depth // piece)
        def _(j):
            columns = pl.ds(pl.multiple_of(j * piece, piece), piece)
            if c == 0:
                acc[:, columns] = product(c, slice(None), columns)
            else:
                acc[:, columns] += product(c, slice(None), columns)

    last = len(cuts) - 1
    pass_on(0)
    for c in range(last):
        pass_on(c + 1)
        arrived(c)
        for b in range(blocks):
            attend(c, b)
        project(c)
    arrived(last)
    w_fill(last).wait()

    def part_to(j, k, peer):
        columns = slice(j * piece, (j + 1) * piece)
        mine = pl.ds(pl.multiple_of(peer * rows, rows), rows)
        return remote(
            sent.at[mine, columns], landed.at[k, :, columns],
            part_send.at[k, j], part_recv.at[k, j], {"head": peer},
        )

    per_block = BLOCK // rows
    for i in range(blocks):
        b = lax.rem(h // per_block + 1 + i, blocks)
        tokens = pl.ds(pl.multiple_of(b * BLOCK, BLOCK), BLOCK)
        attend(last, b)
        for j in range(depth // piece):
            columns = slice(j * piece, (j + 1) * piece)
            total = product(last, tokens, columns)
            if last > 0:
                total = total + acc[tokens, columns]
            sent[tokens, columns] = total.astype(jnp.bfloat16)
            for q in range(per_block):
                peer = b * per_block + q
                if per_block > 1:
                    @pl.when(peer != h)
                    def _():
                        part_to(j, lax.rem(peer - h + heads - 1, heads), peer).start()
                elif i < blocks - 1:
                    part_to(j, lax.rem(peer - h + heads - 1, heads), peer).start()

    own_rows = pl.ds(pl.multiple_of(h * rows, rows), rows)
    for j in range(depth // piece):
        columns = slice(j * piece, (j + 1) * piece)
        total = sent[own_rows, columns].astype(jnp.float32)
        for k in range(heads - 1):
            part_to(j, k, peers[k]).wait_recv()
            total = total + landed[k, :, columns].astype(jnp.float32)
        out_ref[0, :, columns] = total.astype(jnp.bfloat16)

    for c in range(len(cuts)):
        @pl.when(has_right)
        def _():
            to_right(c).wait_send()
            right_sib(c, sib_right).wait_send()

        @pl.when(has_left)
        def _():
            to_left(c).wait_send()
            left_sib(c, sib_left).wait_send()

        @pl.when(inner)
        def _():
            far(c, far_src, far_dst).wait_send()

        own_sib(c, sib_own).wait_send()
        for k in range(heads - 1):
            for copy in fresh_to(c, k):
                copy.wait_send()
    for j in range(depth // piece):
        for k in range(heads - 1):
            part_to(j, k, peers[k]).wait_send()


def per_device(heads, chips, qkv, stale_kv, w_out, neighbors):
    rows = qkv.shape[2]
    tokens = stale_kv.shape[2]
    width, depth = w_out.shape
    blocks = tokens // BLOCK
    cuts = head_cuts(width // HD)
    piece = column_piece(depth)
    pieces = depth // piece
    others = heads - 1
    count = len(cuts)
    bf16 = jnp.bfloat16
    stale = stale_kv.reshape(2, blocks, BLOCK, width)
    slots = (2 * REACH + 1) * blocks
    dma = pltpu.SemaphoreType.DMA
    return pl.pallas_call(
        functools.partial(kernel, heads, chips, cuts, piece),
        out_shape=jax.ShapeDtypeStruct((1, rows, depth), bf16),
        in_specs=[
            pl.BlockSpec(memory_space=pltpu.SMEM),
            pl.BlockSpec(memory_space=pl.ANY),
            pl.BlockSpec(memory_space=pl.ANY),
            pl.BlockSpec(memory_space=pl.ANY),
        ],
        out_specs=pl.BlockSpec(memory_space=pltpu.VMEM),
        scratch_shapes=[
            pltpu.VMEM((width, depth), bf16),
            pltpu.VMEM((tokens, depth), jnp.float32),
            pltpu.VMEM((tokens, width), bf16),
            pltpu.VMEM((tokens, depth), bf16),
            pltpu.VMEM((others, rows, depth), bf16),
            [pltpu.VMEM((2, slots, BLOCK, cut * HD), bf16) for cut in cuts],
            [pltpu.VMEM((tokens, cut * HD), bf16) for cut in cuts],
            dma((3, count)),
            dma((count, others, 2)),
            dma((count, others, 2)),
            dma((count, 3)),
            dma((count, 6)),
            dma((count, 3)),
            dma((others, pieces)),
            dma((others, pieces)),
        ],
        compiler_params=pltpu.CompilerParams(
            collective_id=0, has_side_effects=True, vmem_limit_bytes=62 * 2 ** 20
        ),
        name="windowed",
    )(neighbors, qkv, stale, w_out)


def solution(mesh):
    placed = (
        P(None, ("group", "patch", "sub"), "head", None),
        P(None, ("group", "patch", "sub"), None, "head"),
        P("head", None),
        P(("group", "patch", "sub"), None),
    )
    sizes = dict(mesh.shape)
    return jax.shard_map(
        functools.partial(per_device, sizes["head"], sizes["patch"]),
        mesh=mesh,
        in_specs=placed,
        out_specs=P(("group", "patch", "sub"), "head", None),
        check_vma=False,
    )
```

```python
import functools
import math

import jax
import jax.numpy as jnp
from jax import lax
from jax.experimental import pallas as pl
from jax.experimental.pallas import tpu as pltpu
from jax.sharding import PartitionSpec as P

HD = 128
BLOCK = 64
NB = 6
REACH = 3
MESH = pl.DeviceIdType.MESH


def head_cuts(local_heads):
    if local_heads % 6 == 0:
        return [6] * (local_heads // 6)
    return [1] * local_heads


def column_piece(total):
    for size in (768, 512, 256, 128):
        if total % size == 0:
            return size
    return total


def kernel(
    heads, chips, cuts, piece,
    near_ref, qkv_ref, stale_ref, w_ref, out_ref,
    w_buf, acc, att, sent, landed, banks, asked,
    w_sem, fill_send, fill_recv, own_send, bank_recv, bank_send, part_send, part_recv,
):
    z = lax.axis_index("patch")
    h = lax.axis_index("head")
    s = lax.axis_index("sub")
    row = 2 * z + s
    blocks = stale_ref.shape[1]
    rows = qkv_ref.shape[2]
    width = stale_ref.shape[3]
    depth = out_ref.shape[2]
    has_left = z > 0
    has_right = z < chips - 1
    core0 = s == 0
    has_diag = jnp.logical_or(jnp.logical_and(core0, has_left), jnp.logical_and(s == 1, has_right))
    diag_z = jnp.where(core0, jnp.maximum(z - 1, 0), jnp.minimum(z + 1, chips - 1))
    left = {"patch": jnp.maximum(z - 1, 0)}
    right = {"patch": jnp.minimum(z + 1, chips - 1)}
    sibling = {"sub": 1 - s}
    diag = {"patch": diag_z, "sub": 1 - s}
    peers = [lax.rem(h + k, heads) for k in range(1, heads)]
    sources = [lax.rem(h - k + heads, heads) for k in range(1, heads)]

    barrier = pltpu.get_barrier_semaphore()

    @pl.when(has_left)
    def _():
        pl.semaphore_signal(barrier, inc=1, device_id=left, device_id_type=MESH)

    @pl.when(has_right)
    def _():
        pl.semaphore_signal(barrier, inc=1, device_id=right, device_id_type=MESH)

    @pl.when(has_diag)
    def _():
        pl.semaphore_signal(barrier, inc=1, device_id=diag, device_id_type=MESH)

    pl.semaphore_signal(barrier, inc=1, device_id=sibling, device_id_type=MESH)
    for peer in peers:
        pl.semaphore_signal(barrier, inc=1, device_id={"head": peer}, device_id_type=MESH)

    starts = [sum(cuts[:c]) * HD for c in range(len(cuts))]

    def row_at(c, slot):
        return banks[c].at[:, pl.ds(slot * blocks, blocks)]

    def remote(src, dst, send, recv, device):
        return pltpu.make_async_remote_copy(
            src_ref=src, dst_ref=dst, send_sem=send, recv_sem=recv,
            device_id=device, device_id_type=MESH,
        )

    def fresh_dst(c, owner):
        first = owner * rows
        block = REACH * blocks + first // BLOCK
        inside = pl.multiple_of(first % BLOCK, rows)
        return (
            asked[c].at[pl.ds(pl.multiple_of(first, rows), rows)],
            banks[c].at[:, block, pl.ds(inside, rows)],
        )

    def fresh_src(c, owner):
        cols = pl.ds(pl.multiple_of(owner * width + starts[c], HD), cuts[c] * HD)
        return qkv_ref.at[0, 0, :, cols], qkv_ref.at[1:3, 0, :, cols]

    def local_fill(c):
        src, dst = fresh_src(c, h), fresh_dst(c, h)
        return [pltpu.make_async_copy(src[i], dst[i], w_sem.at[1 + i, c]) for i in range(2)]

    def w_fill(c):
        part = pl.ds(starts[c], cuts[c] * HD)
        return pltpu.make_async_copy(w_ref.at[part], w_buf.at[part], w_sem.at[0, c])

    def fresh_to(c, k):
        src, dst = fresh_src(c, peers[k]), fresh_dst(c, h)
        return [
            remote(src[i], dst[i], fill_send.at[c, k, i], fill_recv.at[c, k, i], {"head": peers[k]})
            for i in range(2)
        ]

    def fresh_from(c, k):
        src, dst = fresh_src(c, h), fresh_dst(c, sources[k])
        return [
            remote(src[i], dst[i], fill_send.at[c, k, i], fill_recv.at[c, k, i], {"head": peers[k]})
            for i in range(2)
        ]

    def own(c):
        return stale_ref.at[:, :, :, starts[c]:starts[c] + cuts[c] * HD]

    def to_right(c):
        return remote(own(c), row_at(c, 1), own_send.at[c, 0], bank_recv.at[c, 0], right)

    def to_left(c):
        return remote(own(c), row_at(c, 5), own_send.at[c, 1], bank_recv.at[c, 1], left)

    sib_own = jnp.where(core0, 2, 4)
    sib_left = jnp.where(core0, 0, 2)
    sib_right = jnp.where(core0, 4, 6)
    my_own = jnp.where(core0, 4, 2)
    my_left = jnp.where(core0, 2, 0)
    my_right = jnp.where(core0, 6, 4)

    def own_sib(c, slot):
        return remote(own(c), row_at(c, slot), own_send.at[c, 2], bank_recv.at[c, 2], sibling)

    def left_sib(c, slot):
        return remote(row_at(c, 1), row_at(c, slot), bank_send.at[c, 0], bank_recv.at[c, 3], sibling)

    def right_sib(c, slot):
        return remote(row_at(c, 5), row_at(c, slot), bank_send.at[c, 1], bank_recv.at[c, 4], sibling)

    def far(c, src, dst):
        return remote(row_at(c, src), row_at(c, dst), bank_send.at[c, 2], bank_recv.at[c, 5], diag)

    inner = jnp.logical_and(has_left, has_right)
    far_src = jnp.where(core0, 5, 1)
    far_dst = jnp.where(core0, 6, 0)
    far_mine = jnp.where(core0, 0, 6)
    has_far = jnp.logical_or(jnp.logical_and(core0, z >= 2), jnp.logical_and(s == 1, z <= chips - 3))

    for c in range(len(cuts)):
        for copy in local_fill(c):
            copy.start()
        w_fill(c).start()

    count = (
        heads + has_left.astype(jnp.int32) + has_right.astype(jnp.int32) + has_diag.astype(jnp.int32)
    )
    pl.semaphore_wait(barrier, count)

    for c in range(len(cuts)):
        @pl.when(has_right)
        def _():
            to_right(c).start()

        @pl.when(has_left)
        def _():
            to_left(c).start()

        for k in range(heads - 1):
            for copy in fresh_to(c, k):
                copy.start()
        own_sib(c, sib_own).start()

    def pass_on(c):
        @pl.when(has_left)
        def _():
            to_left_arrived = remote(own(c), row_at(c, 1), own_send.at[c, 0], bank_recv.at[c, 0], right)
            to_left_arrived.wait_recv()

        @pl.when(has_right)
        def _():
            remote(own(c), row_at(c, 5), own_send.at[c, 1], bank_recv.at[c, 1], left).wait_recv()

        @pl.when(inner)
        def _():
            far(c, far_src, far_dst).start()

        @pl.when(has_left)
        def _():
            left_sib(c, sib_left).start()

        @pl.when(has_right)
        def _():
            right_sib(c, sib_right).start()

    def arrived(c):
        for copy in local_fill(c):
            copy.wait()
        for k in range(heads - 1):
            for copy in fresh_from(c, k):
                copy.wait_recv()
        own_sib(c, my_own).wait_recv()

        @pl.when(has_left)
        def _():
            left_sib(c, my_left).wait_recv()

        @pl.when(has_right)
        def _():
            right_sib(c, my_right).wait_recv()

        @pl.when(has_far)
        def _():
            far(c, far_src, far_mine).wait_recv()

    first_block = (row - REACH) * blocks
    scale = math.log2(math.e) / math.sqrt(HD)

    def attend(c, b):
        tokens = pl.ds(pl.multiple_of(b * BLOCK, BLOCK), BLOCK)
        most = banks[c].shape[1] - 1
        listed = [jnp.clip(near_ref[b, n] - first_block, 0, most) for n in range(NB)]
        spans = [slice(head * HD, (head + 1) * HD) for head in range(cuts[c])]
        scores = [
            lax.dot_general(
                asked[c][tokens, cols],
                jnp.concatenate([banks[c][0, n, :, cols] for n in listed], axis=0),
                (((1,), (1,)), ((), ())),
                preferred_element_type=jnp.float32,
            )
            for cols in spans
        ]
        tops = [jnp.max(score, axis=-1, keepdims=True) for score in scores]
        expos = [jnp.exp2((score - top) * scale) for score, top in zip(scores, tops)]
        sums = [jnp.sum(expo, axis=-1, keepdims=True) for expo in expos]
        expos = [expo * (1.0 / total) for expo, total in zip(expos, sums)]
        got = [
            jnp.dot(
                expo.astype(jnp.bfloat16),
                jnp.concatenate([banks[c][1, n, :, cols] for n in listed], axis=0),
                preferred_element_type=jnp.float32,
            )
            for expo, cols in zip(expos, spans)
        ]
        for head in range(cuts[c]):
            first = starts[c] + head * HD
            att[tokens, first:first + HD] = got[head].astype(jnp.bfloat16)

    def product(c, tokens, columns):
        part = slice(starts[c], starts[c] + cuts[c] * HD)
        return jnp.dot(att[tokens, part], w_buf[part, columns], preferred_element_type=jnp.float32)

    def project(c):
        w_fill(c).wait()

        @pl.loop(0, depth // piece)
        def _(j):
            columns = pl.ds(pl.multiple_of(j * piece, piece), piece)
            if c == 0:
                acc[:, columns] = product(c, slice(None), columns)
            else:
                acc[:, columns] += product(c, slice(None), columns)

    last = len(cuts) - 1
    pass_on(0)
    for c in range(last):
        pass_on(c + 1)
        arrived(c)
        for b in range(blocks):
            attend(c, b)
        project(c)
    arrived(last)
    w_fill(last).wait()

    def part_to(j, k, peer):
        columns = slice(j * piece, (j + 1) * piece)
        mine = pl.ds(pl.multiple_of(peer * rows, rows), rows)
        return remote(
            sent.at[mine, columns], landed.at[k, :, columns],
            part_send.at[k, j], part_recv.at[k, j], {"head": peer},
        )

    per_block = BLOCK // rows
    for i in range(blocks):
        b = lax.rem(h // per_block + 1 + i, blocks)
        tokens = pl.ds(pl.multiple_of(b * BLOCK, BLOCK), BLOCK)
        attend(last, b)
        for j in range(depth // piece):
            columns = slice(j * piece, (j + 1) * piece)
            total = product(last, tokens, columns)
            if last > 0:
                total = total + acc[tokens, columns]
            sent[tokens, columns] = total.astype(jnp.bfloat16)
            for q in range(per_block):
                peer = b * per_block + q
                if per_block > 1:
                    @pl.when(peer != h)
                    def _():
                        part_to(j, lax.rem(peer - h + heads - 1, heads), peer).start()
                elif i < blocks - 1:
                    part_to(j, lax.rem(peer - h + heads - 1, heads), peer).start()

    own_rows = pl.ds(pl.multiple_of(h * rows, rows), rows)
    for j in range(depth // piece):
        columns = slice(j * piece, (j + 1) * piece)
        total = sent[own_rows, columns].astype(jnp.float32)
        for k in range(heads - 1):
            part_to(j, k, peers[k]).wait_recv()
            total = total + landed[k, :, columns].astype(jnp.float32)
        out_ref[0, :, columns] = total.astype(jnp.bfloat16)

    for c in range(len(cuts)):
        @pl.when(has_right)
        def _():
            to_right(c).wait_send()
            right_sib(c, sib_right).wait_send()

        @pl.when(has_left)
        def _():
            to_left(c).wait_send()
            left_sib(c, sib_left).wait_send()

        @pl.when(inner)
        def _():
            far(c, far_src, far_dst).wait_send()

        own_sib(c, sib_own).wait_send()
        for k in range(heads - 1):
            for copy in fresh_to(c, k):
                copy.wait_send()
    for j in range(depth // piece):
        for k in range(heads - 1):
            part_to(j, k, peers[k]).wait_send()


def per_device(heads, chips, qkv, stale_kv, w_out, neighbors):
    rows = qkv.shape[2]
    tokens = stale_kv.shape[2]
    width, depth = w_out.shape
    blocks = tokens // BLOCK
    cuts = head_cuts(width // HD)
    piece = column_piece(depth)
    pieces = depth // piece
    others = heads - 1
    count = len(cuts)
    bf16 = jnp.bfloat16
    stale = stale_kv.reshape(2, blocks, BLOCK, width)
    slots = (2 * REACH + 1) * blocks
    dma = pltpu.SemaphoreType.DMA
    return pl.pallas_call(
        functools.partial(kernel, heads, chips, cuts, piece),
        out_shape=jax.ShapeDtypeStruct((1, rows, depth), bf16),
        in_specs=[
            pl.BlockSpec(memory_space=pltpu.SMEM),
            pl.BlockSpec(memory_space=pl.ANY),
            pl.BlockSpec(memory_space=pl.ANY),
            pl.BlockSpec(memory_space=pl.ANY),
        ],
        out_specs=pl.BlockSpec(memory_space=pltpu.VMEM),
        scratch_shapes=[
            pltpu.VMEM((width, depth), bf16),
            pltpu.VMEM((tokens, depth), jnp.float32),
            pltpu.VMEM((tokens, width), bf16),
            pltpu.VMEM((tokens, depth), bf16),
            pltpu.VMEM((others, rows, depth), bf16),
            [pltpu.VMEM((2, slots, BLOCK, cut * HD), bf16) for cut in cuts],
            [pltpu.VMEM((tokens, cut * HD), bf16) for cut in cuts],
            dma((3, count)),
            dma((count, others, 2)),
            dma((count, others, 2)),
            dma((count, 3)),
            dma((count, 6)),
            dma((count, 3)),
            dma((others, pieces)),
            dma((others, pieces)),
        ],
        compiler_params=pltpu.CompilerParams(
            collective_id=0, has_side_effects=True, vmem_limit_bytes=62 * 2 ** 20
        ),
        name="windowed",
    )(neighbors, qkv, stale, w_out)


def solution(mesh):
    placed = (
        P(None, ("group", "patch", "sub"), "head", None),
        P(None, ("group", "patch", "sub"), None, "head"),
        P("head", None),
        P(("group", "patch", "sub"), None),
    )
    sizes = dict(mesh.shape)
    return jax.shard_map(
        functools.partial(per_device, sizes["head"], sizes["patch"]),
        mesh=mesh,
        in_specs=placed,
        out_specs=P(("group", "patch", "sub"), "head", None),
        check_vma=False,
    )
```

```python
import functools
import math

import jax
import jax.numpy as jnp
from jax import lax
from jax.experimental import pallas as pl
from jax.experimental.pallas import tpu as pltpu
from jax.sharding import PartitionSpec as P

HD = 128
BLOCK = 64
NB = 6
REACH = 3
MESH = pl.DeviceIdType.MESH


def head_cuts(local_heads):
    if local_heads % 6 == 0:
        return [6] * (local_heads // 6)
    return [1] * local_heads


def column_piece(total):
    for size in (768, 512, 256, 128):
        if total % size == 0:
            return size
    return total


def kernel(
    heads, chips, cuts, piece,
    near_ref, qkv_ref, stale_ref, w_ref, out_ref,
    w_buf, acc, att, sent, landed, banks, asked,
    w_sem, fill_send, fill_recv, own_send, bank_recv, bank_send, part_send, part_recv,
):
    z = lax.axis_index("patch")
    h = lax.axis_index("head")
    s = lax.axis_index("sub")
    row = 2 * z + s
    blocks = stale_ref.shape[1]
    rows = qkv_ref.shape[2]
    width = stale_ref.shape[3]
    depth = out_ref.shape[2]
    has_left = z > 0
    has_right = z < chips - 1
    core0 = s == 0
    has_diag = jnp.logical_or(jnp.logical_and(core0, has_left), jnp.logical_and(s == 1, has_right))
    diag_z = jnp.where(core0, jnp.maximum(z - 1, 0), jnp.minimum(z + 1, chips - 1))
    left = {"patch": jnp.maximum(z - 1, 0)}
    right = {"patch": jnp.minimum(z + 1, chips - 1)}
    sibling = {"sub": 1 - s}
    diag = {"patch": diag_z, "sub": 1 - s}
    peers = [lax.rem(h + k, heads) for k in range(1, heads)]
    sources = [lax.rem(h - k + heads, heads) for k in range(1, heads)]

    barrier = pltpu.get_barrier_semaphore()

    @pl.when(has_left)
    def _():
        pl.semaphore_signal(barrier, inc=1, device_id=left, device_id_type=MESH)

    @pl.when(has_right)
    def _():
        pl.semaphore_signal(barrier, inc=1, device_id=right, device_id_type=MESH)

    @pl.when(has_diag)
    def _():
        pl.semaphore_signal(barrier, inc=1, device_id=diag, device_id_type=MESH)

    pl.semaphore_signal(barrier, inc=1, device_id=sibling, device_id_type=MESH)
    for peer in peers:
        pl.semaphore_signal(barrier, inc=1, device_id={"head": peer}, device_id_type=MESH)

    starts = [sum(cuts[:c]) * HD for c in range(len(cuts))]

    def row_at(c, slot):
        return banks[c].at[:, pl.ds(slot * blocks, blocks)]

    def remote(src, dst, send, recv, device):
        return pltpu.make_async_remote_copy(
            src_ref=src, dst_ref=dst, send_sem=send, recv_sem=recv,
            device_id=device, device_id_type=MESH,
        )

    def fresh_dst(c, owner):
        first = owner * rows
        block = REACH * blocks + first // BLOCK
        inside = pl.multiple_of(first % BLOCK, rows)
        return (
            asked[c].at[pl.ds(pl.multiple_of(first, rows), rows)],
            banks[c].at[:, block, pl.ds(inside, rows)],
        )

    def fresh_src(c, owner):
        cols = pl.ds(pl.multiple_of(owner * width + starts[c], HD), cuts[c] * HD)
        return qkv_ref.at[0, 0, :, cols], qkv_ref.at[1:3, 0, :, cols]

    def local_fill(c):
        src, dst = fresh_src(c, h), fresh_dst(c, h)
        return [pltpu.make_async_copy(src[i], dst[i], w_sem.at[1 + i, c]) for i in range(2)]

    def w_fill(c):
        part = pl.ds(starts[c], cuts[c] * HD)
        return pltpu.make_async_copy(w_ref.at[part], w_buf.at[part], w_sem.at[0, c])

    def fresh_to(c, k):
        src, dst = fresh_src(c, peers[k]), fresh_dst(c, h)
        return [
            remote(src[i], dst[i], fill_send.at[c, k, i], fill_recv.at[c, k, i], {"head": peers[k]})
            for i in range(2)
        ]

    def fresh_from(c, k):
        src, dst = fresh_src(c, h), fresh_dst(c, sources[k])
        return [
            remote(src[i], dst[i], fill_send.at[c, k, i], fill_recv.at[c, k, i], {"head": peers[k]})
            for i in range(2)
        ]

    def own(c):
        return stale_ref.at[:, :, :, starts[c]:starts[c] + cuts[c] * HD]

    def to_right(c):
        return remote(own(c), row_at(c, 1), own_send.at[c, 0], bank_recv.at[c, 0], right)

    def to_left(c):
        return remote(own(c), row_at(c, 5), own_send.at[c, 1], bank_recv.at[c, 1], left)

    sib_own = jnp.where(core0, 2, 4)
    sib_left = jnp.where(core0, 0, 2)
    sib_right = jnp.where(core0, 4, 6)
    my_own = jnp.where(core0, 4, 2)
    my_left = jnp.where(core0, 2, 0)
    my_right = jnp.where(core0, 6, 4)

    def own_sib(c, slot):
        return remote(own(c), row_at(c, slot), own_send.at[c, 2], bank_recv.at[c, 2], sibling)

    def left_sib(c, slot):
        return remote(row_at(c, 1), row_at(c, slot), bank_send.at[c, 0], bank_recv.at[c, 3], sibling)

    def right_sib(c, slot):
        return remote(row_at(c, 5), row_at(c, slot), bank_send.at[c, 1], bank_recv.at[c, 4], sibling)

    def far(c, src, dst):
        return remote(row_at(c, src), row_at(c, dst), bank_send.at[c, 2], bank_recv.at[c, 5], diag)

    inner = jnp.logical_and(has_left, has_right)
    far_src = jnp.where(core0, 5, 1)
    far_dst = jnp.where(core0, 6, 0)
    far_mine = jnp.where(core0, 0, 6)
    has_far = jnp.logical_or(jnp.logical_and(core0, z >= 2), jnp.logical_and(s == 1, z <= chips - 3))

    for c in range(len(cuts)):
        for copy in local_fill(c):
            copy.start()
        w_fill(c).start()

    count = (
        heads + has_left.astype(jnp.int32) + has_right.astype(jnp.int32) + has_diag.astype(jnp.int32)
    )
    pl.semaphore_wait(barrier, count)

    for c in range(len(cuts)):
        @pl.when(has_right)
        def _():
            to_right(c).start()

        @pl.when(has_left)
        def _():
            to_left(c).start()

        for k in range(heads - 1):
            for copy in fresh_to(c, k):
                copy.start()
        own_sib(c, sib_own).start()

    def pass_on(c):
        @pl.when(has_left)
        def _():
            to_left_arrived = remote(own(c), row_at(c, 1), own_send.at[c, 0], bank_recv.at[c, 0], right)
            to_left_arrived.wait_recv()

        @pl.when(has_right)
        def _():
            remote(own(c), row_at(c, 5), own_send.at[c, 1], bank_recv.at[c, 1], left).wait_recv()

        @pl.when(inner)
        def _():
            far(c, far_src, far_dst).start()

        @pl.when(has_left)
        def _():
            left_sib(c, sib_left).start()

        @pl.when(has_right)
        def _():
            right_sib(c, sib_right).start()

    def arrived(c):
        for copy in local_fill(c):
            copy.wait()
        for k in range(heads - 1):
            for copy in fresh_from(c, k):
                copy.wait_recv()
        own_sib(c, my_own).wait_recv()

        @pl.when(has_left)
        def _():
            left_sib(c, my_left).wait_recv()

        @pl.when(has_right)
        def _():
            right_sib(c, my_right).wait_recv()

        @pl.when(has_far)
        def _():
            far(c, far_src, far_mine).wait_recv()

    first_block = (row - REACH) * blocks
    scale = math.log2(math.e) / math.sqrt(HD)

    def attend(c, b):
        tokens = pl.ds(pl.multiple_of(b * BLOCK, BLOCK), BLOCK)
        most = banks[c].shape[1] - 1
        listed = [jnp.clip(near_ref[b, n] - first_block, 0, most) for n in range(NB)]
        spans = [slice(head * HD, (head + 1) * HD) for head in range(cuts[c])]
        scores = [
            lax.dot_general(
                asked[c][tokens, cols],
                jnp.concatenate([banks[c][0, n, :, cols] for n in listed], axis=0),
                (((1,), (1,)), ((), ())),
                preferred_element_type=jnp.float32,
            )
            for cols in spans
        ]
        tops = [jnp.max(score, axis=-1, keepdims=True) for score in scores]
        expos = [jnp.exp2((score - top) * scale) for score, top in zip(scores, tops)]
        sums = [jnp.sum(expo, axis=-1, keepdims=True) for expo in expos]
        expos = [expo * (1.0 / total) for expo, total in zip(expos, sums)]
        got = [
            jnp.dot(
                expo.astype(jnp.bfloat16),
                jnp.concatenate([banks[c][1, n, :, cols] for n in listed], axis=0),
                preferred_element_type=jnp.float32,
            )
            for expo, cols in zip(expos, spans)
        ]
        for head in range(cuts[c]):
            first = starts[c] + head * HD
            att[tokens, first:first + HD] = got[head].astype(jnp.bfloat16)

    def product(c, tokens, columns):
        part = slice(starts[c], starts[c] + cuts[c] * HD)
        return jnp.dot(att[tokens, part], w_buf[part, columns], preferred_element_type=jnp.float32)

    def project(c):
        w_fill(c).wait()

        @pl.loop(0, depth // piece)
        def _(j):
            columns = pl.ds(pl.multiple_of(j * piece, piece), piece)
            if c == 0:
                acc[:, columns] = product(c, slice(None), columns)
            else:
                acc[:, columns] += product(c, slice(None), columns)

    last = len(cuts) - 1
    pass_on(0)
    for c in range(last):
        pass_on(c + 1)
        arrived(c)
        for b in range(blocks):
            attend(c, b)
        project(c)
    arrived(last)
    w_fill(last).wait()

    def part_to(j, k, peer):
        columns = slice(j * piece, (j + 1) * piece)
        mine = pl.ds(pl.multiple_of(peer * rows, rows), rows)
        return remote(
            sent.at[mine, columns], landed.at[k, :, columns],
            part_send.at[k, j], part_recv.at[k, j], {"head": peer},
        )

    per_block = BLOCK // rows
    for i in range(blocks):
        b = lax.rem(h // per_block + 1 + i, blocks)
        tokens = pl.ds(pl.multiple_of(b * BLOCK, BLOCK), BLOCK)
        attend(last, b)
        for j in range(depth // piece):
            columns = slice(j * piece, (j + 1) * piece)
            total = product(last, tokens, columns)
            if last > 0:
                total = total + acc[tokens, columns]
            sent[tokens, columns] = total.astype(jnp.bfloat16)
            for q in range(per_block):
                peer = b * per_block + q
                if per_block > 1:
                    @pl.when(peer != h)
                    def _():
                        part_to(j, lax.rem(peer - h + heads - 1, heads), peer).start()
                elif i < blocks - 1:
                    part_to(j, lax.rem(peer - h + heads - 1, heads), peer).start()

    own_rows = pl.ds(pl.multiple_of(h * rows, rows), rows)
    for j in range(depth // piece):
        columns = slice(j * piece, (j + 1) * piece)
        total = sent[own_rows, columns].astype(jnp.float32)
        for k in range(heads - 1):
            part_to(j, k, peers[k]).wait_recv()
            total = total + landed[k, :, columns].astype(jnp.float32)
        out_ref[0, :, columns] = total.astype(jnp.bfloat16)

    for c in range(len(cuts)):
        @pl.when(has_right)
        def _():
            to_right(c).wait_send()
            right_sib(c, sib_right).wait_send()

        @pl.when(has_left)
        def _():
            to_left(c).wait_send()
            left_sib(c, sib_left).wait_send()

        @pl.when(inner)
        def _():
            far(c, far_src, far_dst).wait_send()

        own_sib(c, sib_own).wait_send()
        for k in range(heads - 1):
            for copy in fresh_to(c, k):
                copy.wait_send()
    for j in range(depth // piece):
        for k in range(heads - 1):
            part_to(j, k, peers[k]).wait_send()


def per_device(heads, chips, qkv, stale_kv, w_out, neighbors):
    rows = qkv.shape[2]
    tokens = stale_kv.shape[2]
    width, depth = w_out.shape
    blocks = tokens // BLOCK
    cuts = head_cuts(width // HD)
    piece = column_piece(depth)
    pieces = depth // piece
    others = heads - 1
    count = len(cuts)
    bf16 = jnp.bfloat16
    stale = stale_kv.reshape(2, blocks, BLOCK, width)
    slots = (2 * REACH + 1) * blocks
    dma = pltpu.SemaphoreType.DMA
    return pl.pallas_call(
        functools.partial(kernel, heads, chips, cuts, piece),
        out_shape=jax.ShapeDtypeStruct((1, rows, depth), bf16),
        in_specs=[
            pl.BlockSpec(memory_space=pltpu.SMEM),
            pl.BlockSpec(memory_space=pl.ANY),
            pl.BlockSpec(memory_space=pl.ANY),
            pl.BlockSpec(memory_space=pl.ANY),
        ],
        out_specs=pl.BlockSpec(memory_space=pltpu.VMEM),
        scratch_shapes=[
            pltpu.VMEM((width, depth), bf16),
            pltpu.VMEM((tokens, depth), jnp.float32),
            pltpu.VMEM((tokens, width), bf16),
            pltpu.VMEM((tokens, depth), bf16),
            pltpu.VMEM((others, rows, depth), bf16),
            [pltpu.VMEM((2, slots, BLOCK, cut * HD), bf16) for cut in cuts],
            [pltpu.VMEM((tokens, cut * HD), bf16) for cut in cuts],
            dma((3, count)),
            dma((count, others, 2)),
            dma((count, others, 2)),
            dma((count, 3)),
            dma((count, 6)),
            dma((count, 3)),
            dma((others, pieces)),
            dma((others, pieces)),
        ],
        compiler_params=pltpu.CompilerParams(
            collective_id=0, has_side_effects=True, vmem_limit_bytes=53 * 2 ** 20
        ),
        name="windowed",
    )(neighbors, qkv, stale, w_out)


def solution(mesh):
    placed = (
        P(None, ("group", "patch", "sub"), "head", None),
        P(None, ("group", "patch", "sub"), None, "head"),
        P("head", None),
        P(("group", "patch", "sub"), None),
    )
    sizes = dict(mesh.shape)
    return jax.shard_map(
        functools.partial(per_device, sizes["head"], sizes["patch"]),
        mesh=mesh,
        in_specs=placed,
        out_specs=P(("group", "patch", "sub"), "head", None),
        check_vma=False,
    )
```
